512 devices in a mesh: row: 32 (over x, z_lo, core), col: 16 (over y, z_hi).
Axes of the slice: x: 4, y: 8, z: 8 (z_hi: 2, z_lo: 4; z = z_hi * 4 + z_lo), core: 2. Of those that a mesh axis runs over, the one named last changes fastest.
Arguments:
- omega: bfloat16 [32768, 256], P('row'), may hold values from -6 to 6
- psi: bfloat16 [32768, 256], P('col'), may hold values from -6 to 6
- near_tiles: bfloat16 [32768, 1536], P('row'), may hold values from -0.15625 to 0.15625
- left_factors: bfloat16 [32768, 4096], P('row', 'col'), may hold values from -0.09375 to 0.09375
- right_factors: bfloat16 [4096, 32768], P('row', 'col'), may hold values from -0.25 to 0.25
- admissible: int32 [64, 64], P('row', 'col'), may hold values from 0 to 1, as said below
- ranks: int32 [64, 64], P('row', 'col'), may hold values from 8 to 64, as said below
Outputs:
- samples_right: float32 [32768, 256], P(('row', 'col'))
- samples_left: float32 [32768, 256], P(('col', 'row'))
The draws below stay inside these ranges and needn't reach their ends.
Inputs may be any that keep to these rules, and one draw needn't show every extreme that they name: `admissible`: 0 only where the tiles' indices differ by at most 1; every diagonal tile is 0. `ranks`: some tile has rank 64.
All inputs are finite; a program needn't handle non-finite values.
Results may differ from the reference program's by a relative error of at most 0.0018.
Values may be sent and summed in bfloat16 or wider, within the bound.
A program may use at most 64 MiB of HBM per device.

```python
import jax
import jax.numpy as jnp
from jax import lax

TILE = 512
K = 256
RMAX = 64
NT = 64
N = 32768


def draw_admissible(key, part):
    key = jax.random.fold_in(key, 11)
    places = jnp.arange(NT, dtype=jnp.int32)
    spacing = jnp.abs(places[:, None] - places[None, :])
    coins = jax.random.randint(key, (NT, NT), 0, 2, dtype=jnp.int32)
    return jnp.where(spacing == 0, 0, jnp.where(spacing == 1, coins, 1)).astype(jnp.int32)


def draw_ranks(key, part):
    key = jax.random.fold_in(key, 12)
    first, second = jax.random.split(key)
    values = jax.random.randint(first, (NT * NT,), RMAX // 8, RMAX + 1, dtype=jnp.int32)
    target = jax.random.randint(second, (), 0, NT * NT, dtype=jnp.int32)
    flat = jnp.arange(NT * NT, dtype=jnp.int32)
    return jnp.where(flat == target, RMAX, values).reshape(NT, NT).astype(jnp.int32)


def shard_levels(stream_key, shape, shards, smallest, largest):
    def one(axis_at, blocks):
        draws = jax.random.uniform(jax.random.fold_in(jax.random.fold_in(stream_key, 6), axis_at), (blocks,), jnp.float32, smallest / len(shards), largest / len(shards))
        return jnp.repeat(jnp.exp(draws), shape[axis_at] // blocks).reshape((-1,) + (1,) * (len(shape) - axis_at - 1))

    level = one(*shards[0])
    for cut in shards[1:]:
        level = level * one(*cut)
    return level


def bell_draw(stream_key, extent, width, most, cuts=(), kind=jnp.bfloat16):
    values = width * jax.random.normal(stream_key, extent, jnp.float32)
    if cuts:
        values = values * shard_levels(stream_key, extent, cuts, -0.22, 0.18)
    return jnp.clip(values, -most, most).astype(kind)


def setup_inputs(seed: int = 0) -> dict:
    key_list = jax.random.split(jax.random.key(seed), 8)
    omega = bell_draw(key_list[0], (N, K), 1.0, 6.0, ((0, 32),))
    psi = bell_draw(key_list[1], (N, K), 1.0, 6.0, ((0, 16),))
    near_tiles = bell_draw(key_list[2], (N, 3 * TILE), (3 * TILE) ** -0.5, 0.15625, ((0, 32),))
    left_factors = bell_draw(key_list[3], (N, NT * RMAX), (RMAX * NT) ** -0.5, 0.09375, ((0, 32), (1, 16)))
    right_factors = bell_draw(key_list[4], (NT * RMAX, N), TILE ** -0.5, 0.25, ((0, 32), (1, 16)))
    admissible = draw_admissible(jax.random.fold_in(key_list[7], 71), 0)
    ranks = draw_ranks(jax.random.fold_in(key_list[7], 71), 0)
    return {"omega": omega, "psi": psi, "near_tiles": near_tiles, "left_factors": left_factors, "right_factors": right_factors, "admissible": admissible, "ranks": ranks}


def reference(omega, psi, near_tiles, left_factors, right_factors, admissible, ranks):
    om = omega.astype(jnp.float32).reshape(NT, TILE, K)
    ps = psi.astype(jnp.float32).reshape(NT, TILE, K)
    edge = jnp.zeros((1, TILE, K), jnp.float32)
    om_pad = jnp.concatenate([edge, om, edge], axis=0)
    levels = jnp.arange(RMAX, dtype=jnp.int32)
    ones = jnp.ones((1,), jnp.int32)

    def step(zpad, i):
        ub = lax.dynamic_slice_in_dim(left_factors, i * TILE, TILE, 0).astype(jnp.float32).reshape(TILE, NT, RMAX)
        vb = lax.dynamic_slice_in_dim(right_factors, i * RMAX, RMAX, 0).astype(jnp.float32).reshape(RMAX, NT, TILE)
        adm_row = lax.dynamic_index_in_dim(admissible, i, 0, keepdims=False)
        rank_row = lax.dynamic_index_in_dim(ranks, i, 0, keepdims=False)
        keep = ((levels[None, :] < rank_row[:, None]) & (adm_row[:, None] == 1)).astype(jnp.float32)
        coeff = (jnp.einsum('rjt,jtk->jrk', vb, om) * keep[:, :, None]).astype(jnp.bfloat16)
        coeff = lax.optimization_barrier(coeff).astype(jnp.float32)
        yrow = jnp.einsum('tjr,jrk->tk', ub, coeff)
        p_i = lax.dynamic_index_in_dim(ps, i, 0, keepdims=False)
        left_coeff = (jnp.einsum('tjr,tk->jrk', ub, p_i) * keep[:, :, None]).astype(jnp.bfloat16)
        left_coeff = lax.optimization_barrier(left_coeff).astype(jnp.float32)
        zadd = jnp.einsum('rjt,jrk->jtk', vb, left_coeff)
        strip = lax.dynamic_slice_in_dim(near_tiles, i * TILE, TILE, 0).astype(jnp.float32).reshape(TILE, 3, TILE)
        band = lax.dynamic_slice_in_dim(om_pad, i, 3, 0)
        adm_pad = jnp.concatenate([ones, adm_row, ones])
        flags = (lax.dynamic_slice_in_dim(adm_pad, i, 3, 0) == 0).astype(jnp.float32)
        yrow = yrow + jnp.einsum('tos,osk->tk', strip * flags[None, :, None], band)
        dense_z = jnp.einsum('tos,tk->osk', strip, p_i) * flags[:, None, None]
        zpad = zpad.at[1:NT + 1].add(zadd)
        current = lax.dynamic_slice_in_dim(zpad, i, 3, 0)
        zpad = lax.dynamic_update_slice_in_dim(zpad, current + dense_z, i, 0)
        return zpad, yrow

    zpad, rows = lax.scan(step, jnp.zeros((NT + 2, TILE, K), jnp.float32), jnp.arange(NT, dtype=jnp.int32))
    return rows.reshape(N, K), zpad[1:NT + 1].reshape(N, K)
```

```python
import jax
import jax.numpy as jnp
from jax import lax
from jax.experimental import pallas as pl
from jax.experimental.pallas import tpu as pltpu
from jax.sharding import PartitionSpec as P

MESH = pl.DeviceIdType.MESH
TILE = 512
K = 256
RMAX = 64
F32 = jnp.float32
BF16 = jnp.bfloat16


def device(x, zl, k, y, zh):
    return (x * 8 + zl * 2 + k, y * 2 + zh)


def psi_source(z):
    return jnp.where(z == 4, 3, jnp.where(z == 3, 4, jnp.where(z == 6, 1, jnp.where(z == 1, 6, z))))


def parent(q, root):
    return jnp.where((root == 0) & (q == 3), 2, jnp.where((root == 3) & (q == 0), 1, root))


def kernel(omega, psi, near, left, right, adm, ranks, y_out, z_out,
           om, ps, nr, uu, vv, cr, cl, yp, y16, yr, yacc, yh, zp, zc, z16, zr,
           load_sem, ps_send, ps_recv, om_send, om_recv, tw_send, tw_recv,
           y_send, y_recv, h_send, h_recv, c_send, c_recv, z_send, z_recv):
    row = lax.axis_index("row")
    col = lax.axis_index("col")
    x, zl, k = row // 8, (row // 2) % 4, row % 2
    y, zh = col // 2, col % 2
    z = zh * 4 + zl
    place = row // 2

    xs, qs = y // 2, (y % 2) * 2 + zh
    ps_y = 2 * x + zl // 2
    ps_z = psi_source(z)
    tz = psi_source(z)
    tx = y // 2
    serves = (tz % 4) == (y % 2) * 2 + zh
    om_root = (x == xs) & (zl == qs)
    first = k == 0

    def remote(src, dst, ss, rs, dev):
        return pltpu.make_async_remote_copy(src_ref=src, dst_ref=dst, send_sem=ss, recv_sem=rs,
                                            device_id=dev, device_id_type=MESH)

    om_from_x = jnp.where(first, zl == qs, x != xs) & ~om_root
    om_from_z = jnp.where(first, zl != qs, (x == xs) & (zl != qs))
    sends_x = jnp.where(first, om_root, x == xs)
    may_send_z = jnp.where(first, True, x == xs)

    barrier = pltpu.get_barrier_semaphore()

    def greet(dev):
        pl.semaphore_signal(barrier, inc=1, device_id=dev, device_id_type=MESH)

    count = 0
    for i in range(4):
        mine = (x == i) & (y == ps_y) & (z == ps_z)

        @pl.when(jnp.logical_not(mine))
        def _(i=i):
            greet(device(i, ps_z % 4, k, ps_y, ps_z // 4))
    for i in range(8):
        other = serves & jnp.logical_not((x == tx) & (y == i) & (z == tz))
        count += jnp.where(other, 1, 0)

    @pl.when(om_from_x)
    def _():
        greet(device(xs, zl, k, y, zh))

    @pl.when(om_from_z)
    def _():
        greet(device(x, parent(zl, qs), k, y, zh))
    count += jnp.where(sends_x, 3, 0)
    for q in range(4):
        child = may_send_z & (q != qs) & (parent(q, qs) == zl)
        count += jnp.where(child, 1, 0)
    greet(device(x, zl, 1 - k, y, zh))
    for i in range(1, 8):
        greet(device(x, zl, k, (y + i) % 8, zh))
    greet(device(x, zl, k, y, 1 - zh))
    for i in range(1, 16):
        p = (place + i) % 16
        greet(device(p // 4, p % 4, k, y, zh))
    count += 1 + 7 + 1 + 15

    loads = [pltpu.make_async_copy(right, vv, load_sem.at[0]),
             pltpu.make_async_copy(left, uu, load_sem.at[1]),
             pltpu.make_async_copy(near, nr, load_sem.at[2])]
    for c in loads:
        c.start()
    pl.semaphore_wait(barrier, count)

    ps_sends = []
    for i in range(8):
        other = serves & jnp.logical_not((x == tx) & (y == i) & (z == tz))
        src = psi.at[pl.ds(pl.multiple_of(k * 1024 + x * 256, 256), 256)]
        dst = ps.at[pl.ds(pl.multiple_of(x * 256, 256), 256)]
        ps_sends.append((other, remote(src, dst, ps_send.at[i], ps_recv.at[x],
                                       device(tx, tz % 4, k, i, tz // 4))))
    own_psi = serves & (x == tx) & (z == tz)
    own_copy = pltpu.make_async_copy(psi.at[pl.ds(pl.multiple_of(k * 1024 + x * 256, 256), 256)],
                                     ps.at[pl.ds(pl.multiple_of(x * 256, 256), 256)], load_sem.at[3])

    slot = om.at[k]

    @pl.when(om_root)
    def _():
        c = pltpu.make_async_copy(omega, slot, load_sem.at[4])
        c.start()
        c.wait()

    for cond, c in ps_sends:
        @pl.when(cond)
        def _(c=c):
            c.start()

    @pl.when(own_psi)
    def _():
        own_copy.start()

    @pl.when(jnp.logical_not(om_root))
    def _():
        remote(slot, slot, om_send.at[0], om_recv, device(x, zl, 1 - k, y, zh)).wait_recv()

    om_sends = []
    for i in range(1, 4):
        om_sends.append((sends_x, remote(slot, slot, om_send.at[i - 1], om_recv,
                                         device((x + i) % 4, zl, k, y, zh))))
    for q in range(4):
        child = may_send_z & (q != qs) & (parent(q, qs) == zl)
        om_sends.append((child, remote(slot, slot, om_send.at[3 + q], om_recv, device(x, q, k, y, zh))))
    for cond, c in om_sends:
        @pl.when(cond)
        def _(c=c):
            c.start()
    twin = remote(slot, slot, tw_send, tw_recv, device(x, zl, 1 - k, y, zh))
    twin.start()

    for c in loads:
        c.wait()

    level = lax.broadcasted_iota(jnp.int32, (RMAX, K), 0)

    def limit(a, b):
        return jnp.where(adm[a, b] == 1, ranks[a, b], 0)

    def flag(a, b):
        return jnp.where(adm[a, b] == 0, 1.0, 0.0).astype(F32)

    for i in range(4):
        mine = (x == i) & own_psi

        @pl.when(jnp.logical_not(mine & (y == ps_y)))
        def _(i=i):
            part = ps.at[pl.ds(i * 256, 256)]
            remote(part, part, ps_send.at[0], ps_recv.at[i], device(x, zl, 1 - k, y, zh)).wait_recv()

    @pl.when(own_psi)
    def _():
        own_copy.wait()

    for a in range(2):
        full = lax.dot_general(uu[a * TILE:(a + 1) * TILE, :], ps[a * TILE:(a + 1) * TILE, :],
                               (((0,), (0,)), ((), ())), preferred_element_type=F32)
        for b in range(4):
            piece = full[b * RMAX:(b + 1) * RMAX]
            cl[b, a * RMAX:(a + 1) * RMAX, :] = jnp.where(level < limit(a, b), piece, 0.0).astype(BF16)
    core_sends = []
    for b in range(4):
        part = lax.dot_general(vv[:, b * TILE:(b + 1) * TILE], cl[b], (((0,), (0,)), ((), ())),
                               preferred_element_type=F32)
        zp[4 * b:4 * b + 4] = part.reshape(4, 2, 64, K)
        for a in range(2):
            off = 4 * col + b - (2 * row + a) + 1

            @pl.when((off >= 0) & (off <= 2))
            def _(a=a, b=b, off=off):
                block = nr[a * TILE:(a + 1) * TILE, pl.ds(pl.multiple_of(off * TILE, TILE), TILE)]
                add = lax.dot_general(block, ps[a * TILE:(a + 1) * TILE, :], (((0,), (0,)), ((), ())),
                                      preferred_element_type=F32)
                zp[4 * b:4 * b + 4] += (add * flag(a, b)).reshape(4, 2, 64, K)
        c = remote(zp.at[pl.ds(4 * b, 4), 1 - k], zc.at[pl.ds(4 * b, 4)], c_send.at[b], c_recv.at[b],
                   device(x, zl, 1 - k, y, zh))
        c.start()
        core_sends.append(c)
    for b in range(4):
        core_sends[b].wait_recv()
        zc[4 * b:4 * b + 4] = zc[4 * b:4 * b + 4] + zp[4 * b:4 * b + 4, k]
        z16[4 * b:4 * b + 4] = zc[4 * b:4 * b + 4].astype(BF16)
    z_sends = []
    for i in range(1, 16):
        p = (place + i) % 16
        c = remote(z16.at[p], zr.at[place], z_send.at[i], z_recv.at[place], device(p // 4, p % 4, k, y, zh))
        c.start()
        z_sends.append(c)

    twin.wait_recv()
    for b in range(4):
        half = om.at[b // 2]
        full = jnp.dot(vv[:, b * TILE:(b + 1) * TILE], half[(b % 2) * TILE:(b % 2 + 1) * TILE, :],
                       preferred_element_type=F32)
        for a in range(2):
            piece = full[a * RMAX:(a + 1) * RMAX]
            cr[a, b * RMAX:(b + 1) * RMAX, :] = jnp.where(level < limit(a, b), piece, 0.0).astype(BF16)
    y_sends = []
    for a in range(2):
        yp[4 * a:4 * a + 4] = jnp.dot(uu[a * TILE:(a + 1) * TILE, :], cr[a],
                                      preferred_element_type=F32).reshape(4, 128, K)
        for b in range(4):
            off = 4 * col + b - (2 * row + a) + 1

            @pl.when((off >= 0) & (off <= 2))
            def _(a=a, b=b, off=off):
                block = nr[a * TILE:(a + 1) * TILE, pl.ds(pl.multiple_of(off * TILE, TILE), TILE)]
                add = jnp.dot(block, om[b // 2, (b % 2) * TILE:(b % 2 + 1) * TILE, :],
                              preferred_element_type=F32)
                yp[4 * a:4 * a + 4] += (add * flag(a, b)).reshape(4, 128, K)
        y16[4 * a:4 * a + 4] = yp[4 * a:4 * a + 4].astype(BF16)
    for i in range(1, 8):
        p = (y + i) % 8
        c = remote(y16.at[p], yr.at[y], y_send.at[i], y_recv.at[y], device(x, zl, k, p, zh))
        c.start()
        y_sends.append(c)

    total = yp[y]
    for i in range(1, 8):
        p = (y + i) % 8
        remote(y16.at[p], yr.at[p], y_send.at[i], y_recv.at[p], device(x, zl, k, p, zh)).wait_recv()
        total += yr[p].astype(F32)
    yacc[...] = total.reshape(2, 64, K)
    across = remote(yacc.at[1 - zh], yh, h_send, h_recv, device(x, zl, k, y, 1 - zh))
    across.start()

    ztot = zc[place]
    for i in range(1, 16):
        p = (place + i) % 16
        remote(z16.at[p], zr.at[p], z_send.at[i], z_recv.at[p], device(p // 4, p % 4, k, y, zh)).wait_recv()
        ztot += zr[p].astype(F32)
    z_out[...] = ztot

    across.wait_recv()
    y_out[...] = yacc[zh] + yh[...]

    for cond, c in ps_sends + om_sends:
        @pl.when(cond)
        def _(c=c):
            c.wait_send()
    twin.wait_send()
    across.wait_send()
    for c in core_sends + z_sends + y_sends:
        c.wait_send()


def local(omega, psi, near_tiles, left_factors, right_factors, admissible, ranks):
    dma = pltpu.SemaphoreType.DMA
    anywhere = pl.BlockSpec(memory_space=pl.ANY)
    scalars = pl.BlockSpec(memory_space=pltpu.SMEM)
    vmem = pl.BlockSpec(memory_space=pltpu.VMEM)
    out = jax.ShapeDtypeStruct((64, K), F32)
    return pl.pallas_call(
        kernel,
        out_shape=(out, out),
        in_specs=[anywhere] * 5 + [scalars] * 2,
        out_specs=(vmem, vmem),
        scratch_shapes=[
            pltpu.VMEM((2, 1024, K), BF16),
            pltpu.VMEM((1024, K), BF16),
            pltpu.VMEM((1024, 3 * TILE), BF16),
            pltpu.VMEM((1024, 256), BF16),
            pltpu.VMEM((128, 2048), BF16),
            pltpu.VMEM((2, 256, K), BF16),
            pltpu.VMEM((4, 128, K), BF16),
            pltpu.VMEM((8, 128, K), F32),
            pltpu.VMEM((8, 128, K), BF16),
            pltpu.VMEM((8, 128, K), BF16),
            pltpu.VMEM((2, 64, K), F32),
            pltpu.VMEM((64, K), F32),
            pltpu.VMEM((16, 2, 64, K), F32),
            pltpu.VMEM((16, 64, K), F32),
            pltpu.VMEM((16, 64, K), BF16),
            pltpu.VMEM((16, 64, K), BF16),
            dma((5,)), dma((8,)), dma((4,)), dma((7,)), dma, dma, dma,
            dma((8,)), dma((8,)), dma, dma, dma((4,)), dma((4,)), dma((16,)), dma((16,)),
        ],
        compiler_params=pltpu.CompilerParams(collective_id=0, has_side_effects=True,
                                             vmem_limit_bytes=48 << 20),
        cost_estimate=pl.CostEstimate(flops=2 * 10 ** 9, bytes_accessed=6 << 20, transcendentals=0),
    )(omega, psi, near_tiles, left_factors, right_factors, admissible, ranks)


def solution(mesh):
    return jax.shard_map(
        local,
        mesh=mesh,
        in_specs=(
            P("row", None),
            P("col", None),
            P("row", None),
            P("row", "col"),
            P("row", "col"),
            P("row", "col"),
            P("row", "col"),
        ),
        out_specs=(P(("row", "col"), None), P(("col", "row"), None)),
        check_vma=False,
    )
```

```python
import jax
import jax.numpy as jnp
from jax import lax
from jax.experimental import pallas as pl
from jax.experimental.pallas import tpu as pltpu
from jax.sharding import PartitionSpec as P

MESH = pl.DeviceIdType.MESH
TILE = 512
K = 256
RMAX = 64
F32 = jnp.float32
BF16 = jnp.bfloat16


def device(x, zl, k, y, zh):
    return (x * 8 + zl * 2 + k, y * 2 + zh)


def psi_source(z):
    return jnp.where(z == 4, 3, jnp.where(z == 3, 4, jnp.where(z == 6, 1, jnp.where(z == 1, 6, z))))


def kernel(omega, psi, near, left, right, adm_in, ranks_in, y_out, z_out,
           om, ps, nr, uu, vv, cr, cl, yp, y16, yr, yacc, yh, zp, zc, z16, zr,
           adm, ranks, load_sem, ps_send, ps_recv, om_send, om_recv, tw_send, tw_recv,
           y_send, y_recv, h_send, h_recv, c_send, c_recv, z_send, z_recv):
    row = lax.axis_index("row")
    col = lax.axis_index("col")
    x, zl, k = row // 8, (row // 2) % 4, row % 2
    y, zh = col // 2, col % 2
    z = zh * 4 + zl
    place = row // 2

    xs, qs = y // 2, (y % 2) * 2 + zh
    ps_y = 2 * x + zl // 2
    ps_z = psi_source(z)
    tz = psi_source(z)
    tx = y // 2
    serves = (tz % 4) == (y % 2) * 2 + zh
    om_root = (x == xs) & (zl == qs)
    first = k == 0

    def remote(src, dst, ss, rs, dev):
        return pltpu.make_async_remote_copy(src_ref=src, dst_ref=dst, send_sem=ss, recv_sem=rs,
                                            device_id=dev, device_id_type=MESH)

    u, v = jnp.where(first, x, zl), jnp.where(first, zl, x)
    us, vs = jnp.where(first, xs, qs), jnp.where(first, qs, xs)
    on_axis = v == vs

    def at(a, b):
        return device(jnp.where(first, a, b), jnp.where(first, b, a), k, y, zh)

    barrier = pltpu.get_barrier_semaphore()

    def greet(dev):
        pl.semaphore_signal(barrier, inc=1, device_id=dev, device_id_type=MESH)

    count = 0
    for i in range(4):
        mine = (x == i) & (y == ps_y) & (z == ps_z)

        @pl.when(jnp.logical_not(mine))
        def _(i=i):
            greet(device(i, ps_z % 4, k, ps_y, ps_z // 4))
    for i in range(8):
        other = serves & jnp.logical_not((x == tx) & (y == i) & (z == tz))
        count += jnp.where(other, 1, 0)

    @pl.when(on_axis & (u != us))
    def _():
        greet(at(us, vs))

    @pl.when(jnp.logical_not(on_axis))
    def _():
        greet(at(u, vs))

    @pl.when(jnp.logical_not(om_root))
    def _():
        for i in range(1, 4):
            greet(at((u + i) % 4, v))
    count += jnp.where(om_root, 3, 0) + jnp.where(on_axis, 3, 0)
    count += jnp.where(on_axis & (u != us), 2, 3)
    greet(device(x, zl, 1 - k, y, zh))
    for i in range(1, 8):
        greet(device(x, zl, k, (y + i) % 8, zh))
    greet(device(x, zl, k, y, 1 - zh))
    for i in range(1, 16):
        p = (place + i) % 16
        greet(device(p // 4, p % 4, k, y, zh))
    count += 1 + 7 + 1 + 15

    loads = [pltpu.make_async_copy(right, vv, load_sem.at[0]),
             pltpu.make_async_copy(left, uu, load_sem.at[1]),
             pltpu.make_async_copy(near, nr, load_sem.at[2]),
             pltpu.make_async_copy(adm_in, adm, load_sem.at[5]),
             pltpu.make_async_copy(ranks_in, ranks, load_sem.at[6])]
    root_copy = pltpu.make_async_copy(omega, om.at[k], load_sem.at[4])

    @pl.when(om_root)
    def _():
        root_copy.start()
    for c in loads:
        c.start()
    pl.semaphore_wait(barrier, count)

    @pl.when(om_root)
    def _():
        root_copy.wait()

    ps_sends = []
    for i in range(8):
        other = serves & jnp.logical_not((x == tx) & (y == i) & (z == tz))
        src = psi.at[pl.ds(pl.multiple_of(k * 1024 + x * 256, 256), 256)]
        dst = ps.at[pl.ds(pl.multiple_of(x * 256, 256), 256)]
        ps_sends.append((other, remote(src, dst, ps_send.at[i], ps_recv.at[x],
                                       device(tx, tz % 4, k, i, tz // 4))))
    own_psi = serves & (x == tx) & (z == tz)
    own_copy = pltpu.make_async_copy(psi.at[pl.ds(pl.multiple_of(k * 1024 + x * 256, 256), 256)],
                                     ps.at[pl.ds(pl.multiple_of(x * 256, 256), 256)], load_sem.at[3])

    slot = om.at[k]

    def quarter(j):
        return slot.at[pl.ds(pl.multiple_of(j * 256, 256), 256)]

    for cond, c in ps_sends:
        @pl.when(cond)
        def _(c=c):
            c.start()

    @pl.when(own_psi)
    def _():
        own_copy.start()

    om_sends = []

    def send_omega(cond, j, sem, dev):
        c = remote(quarter(j), quarter(j), om_send.at[sem], om_recv.at[j], dev)
        om_sends.append((cond, c))

        @pl.when(cond)
        def _():
            c.start()

    def omega_arrived(j):
        remote(quarter(j), quarter(j), om_send.at[0], om_recv.at[j], device(x, zl, 1 - k, y, zh)).wait_recv()

    for i in range(1, 4):
        j = (us + i) % 4
        send_omega(om_root, j, i - 1, at(j, vs))

    @pl.when(jnp.logical_not(om_root))
    def _():
        omega_arrived(u)
    for i in range(1, 4):
        send_omega(on_axis, u, 2 + i, at(u, (v + i) % 4))
    for i in range(1, 4):
        j = (u + i) % 4
        send_omega(jnp.logical_not(on_axis & (j == us)), u, 5 + i, at(j, v))
    twins = []
    for i in range(4):
        j = (u + i) % 4
        if i:
            @pl.when(jnp.logical_not(om_root))
            def _(j=j):
                omega_arrived(j)
        c = remote(quarter(j), quarter(j), tw_send.at[j], tw_recv.at[j], device(x, zl, 1 - k, y, zh))
        c.start()
        twins.append(c)

    for c in loads:
        c.wait()

    level = lax.broadcasted_iota(jnp.int32, (RMAX, K), 0)

    def limit(a, b):
        return jnp.where(adm[a, b] == 1, ranks[a, b], 0)

    def flag(a, b):
        return jnp.where(adm[a, b] == 0, 1.0, 0.0).astype(F32)

    for i in range(4):
        mine = (x == i) & own_psi

        @pl.when(jnp.logical_not(mine & (y == ps_y)))
        def _(i=i):
            part = ps.at[pl.ds(i * 256, 256)]
            remote(part, part, ps_send.at[0], ps_recv.at[i], device(x, zl, 1 - k, y, zh)).wait_recv()

    @pl.when(own_psi)
    def _():
        own_copy.wait()

    for a in range(2):
        full = lax.dot_general(uu[a * TILE:(a + 1) * TILE, :], ps[a * TILE:(a + 1) * TILE, :],
                               (((0,), (0,)), ((), ())), preferred_element_type=F32)
        for b in range(4):
            piece = full[b * RMAX:(b + 1) * RMAX]
            cl[b, a * RMAX:(a + 1) * RMAX, :] = jnp.where(level < limit(a, b), piece, 0.0).astype(BF16)
    core_sends = []
    for b in range(4):
        part = lax.dot_general(vv[:, b * TILE:(b + 1) * TILE], cl[b], (((0,), (0,)), ((), ())),
                               preferred_element_type=F32)
        zp[4 * b:4 * b + 4] = part.reshape(4, 2, 64, K)
        for a in range(2):
            off = 4 * col + b - (2 * row + a) + 1

            @pl.when((off >= 0) & (off <= 2))
            def _(a=a, b=b, off=off):
                block = nr[a * TILE:(a + 1) * TILE, pl.ds(pl.multiple_of(off * TILE, TILE), TILE)]
                add = lax.dot_general(block, ps[a * TILE:(a + 1) * TILE, :], (((0,), (0,)), ((), ())),
                                      preferred_element_type=F32)
                zp[4 * b:4 * b + 4] += (add * flag(a, b)).reshape(4, 2, 64, K)
        c = remote(zp.at[pl.ds(4 * b, 4), 1 - k], zc.at[pl.ds(4 * b, 4)], c_send.at[b], c_recv.at[b],
                   device(x, zl, 1 - k, y, zh))
        c.start()
        core_sends.append(c)
    for b in range(4):
        core_sends[b].wait_recv()
        zc[4 * b:4 * b + 4] = zc[4 * b:4 * b + 4] + zp[4 * b:4 * b + 4, k]
        z16[4 * b:4 * b + 4] = zc[4 * b:4 * b + 4].astype(BF16)
    z_sends = []
    for i in range(1, 16):
        p = (place + i) % 16
        c = remote(z16.at[p], zr.at[place], z_send.at[i], z_recv.at[place], device(p // 4, p % 4, k, y, zh))
        c.start()
        z_sends.append(c)

    other_half = om.at[1 - k]
    for j in range(4):
        part = other_half.at[pl.ds(256 * j, 256)]
        remote(part, part, tw_send.at[j], tw_recv.at[j], device(x, zl, 1 - k, y, zh)).wait_recv()
    for b in range(4):
        half = om.at[b // 2]
        full = jnp.dot(vv[:, b * TILE:(b + 1) * TILE], half[(b % 2) * TILE:(b % 2 + 1) * TILE, :],
                       preferred_element_type=F32)
        for a in range(2):
            piece = full[a * RMAX:(a + 1) * RMAX]
            cr[a, b * RMAX:(b + 1) * RMAX, :] = jnp.where(level < limit(a, b), piece, 0.0).astype(BF16)
    y_sends = []
    for a in range(2):
        yp[4 * a:4 * a + 4] = jnp.dot(uu[a * TILE:(a + 1) * TILE, :], cr[a],
                                      preferred_element_type=F32).reshape(4, 128, K)
        for b in range(4):
            off = 4 * col + b - (2 * row + a) + 1

            @pl.when((off >= 0) & (off <= 2))
            def _(a=a, b=b, off=off):
                block = nr[a * TILE:(a + 1) * TILE, pl.ds(pl.multiple_of(off * TILE, TILE), TILE)]
                add = jnp.dot(block, om[b // 2, (b % 2) * TILE:(b % 2 + 1) * TILE, :],
                              preferred_element_type=F32)
                yp[4 * a:4 * a + 4] += (add * flag(a, b)).reshape(4, 128, K)
        y16[4 * a:4 * a + 4] = yp[4 * a:4 * a + 4].astype(BF16)
    for i in range(1, 8):
        p = (y + i) % 8
        c = remote(y16.at[p], yr.at[y], y_send.at[i], y_recv.at[y], device(x, zl, k, p, zh))
        c.start()
        y_sends.append(c)

    total = yp[y]
    for i in range(1, 8):
        p = (y + i) % 8
        remote(y16.at[p], yr.at[p], y_send.at[i], y_recv.at[p], device(x, zl, k, p, zh)).wait_recv()
        total += yr[p].astype(F32)
    yacc[...] = total.reshape(2, 64, K)
    across = remote(yacc.at[1 - zh], yh, h_send, h_recv, device(x, zl, k, y, 1 - zh))
    across.start()

    ztot = zc[place]
    for i in range(1, 16):
        p = (place + i) % 16
        remote(z16.at[p], zr.at[p], z_send.at[i], z_recv.at[p], device(p // 4, p % 4, k, y, zh)).wait_recv()
        ztot += zr[p].astype(F32)
    z_out[...] = ztot

    across.wait_recv()
    y_out[...] = yacc[zh] + yh[...]

    for cond, c in ps_sends + om_sends:
        @pl.when(cond)
        def _(c=c):
            c.wait_send()
    across.wait_send()
    for c in twins + core_sends + z_sends + y_sends:
        c.wait_send()


def local(omega, psi, near_tiles, left_factors, right_factors, admissible, ranks):
    dma = pltpu.SemaphoreType.DMA
    anywhere = pl.BlockSpec(memory_space=pl.ANY)
    vmem = pl.BlockSpec(memory_space=pltpu.VMEM)
    out = jax.ShapeDtypeStruct((64, K), F32)
    return pl.pallas_call(
        kernel,
        out_shape=(out, out),
        in_specs=[anywhere] * 7,
        out_specs=(vmem, vmem),
        scratch_shapes=[
            pltpu.VMEM((2, 1024, K), BF16),
            pltpu.VMEM((1024, K), BF16),
            pltpu.VMEM((1024, 3 * TILE), BF16),
            pltpu.VMEM((1024, 256), BF16),
            pltpu.VMEM((128, 2048), BF16),
            pltpu.VMEM((2, 256, K), BF16),
            pltpu.VMEM((4, 128, K), BF16),
            pltpu.VMEM((8, 128, K), F32),
            pltpu.VMEM((8, 128, K), BF16),
            pltpu.VMEM((8, 128, K), BF16),
            pltpu.VMEM((2, 64, K), F32),
            pltpu.VMEM((64, K), F32),
            pltpu.VMEM((16, 2, 64, K), F32),
            pltpu.VMEM((16, 64, K), F32),
            pltpu.VMEM((16, 64, K), BF16),
            pltpu.VMEM((16, 64, K), BF16),
            pltpu.SMEM((2, 4), jnp.int32),
            pltpu.SMEM((2, 4), jnp.int32),
            dma((7,)), dma((8,)), dma((4,)), dma((9,)), dma((4,)), dma((4,)), dma((4,)),
            dma((8,)), dma((8,)), dma, dma, dma((4,)), dma((4,)), dma((16,)), dma((16,)),
        ],
        compiler_params=pltpu.CompilerParams(collective_id=0, has_side_effects=True,
                                             vmem_limit_bytes=64 << 20),
        cost_estimate=pl.CostEstimate(flops=2 * 10 ** 9, bytes_accessed=6 << 20, transcendentals=0),
    )(omega, psi, near_tiles, left_factors, right_factors, admissible, ranks)


def solution(mesh):
    return jax.shard_map(
        local,
        mesh=mesh,
        in_specs=(
            P("row", None),
            P("col", None),
            P("row", None),
            P("row", "col"),
            P("row", "col"),
            P("row", "col"),
            P("row", "col"),
        ),
        out_specs=(P(("row", "col"), None), P(("col", "row"), None)),
        check_vma=False,
    )
```

```python
import jax
import jax.numpy as jnp
from jax import lax
from jax.experimental import pallas as pl
from jax.experimental.pallas import tpu as pltpu
from jax.sharding import PartitionSpec as P

MESH = pl.DeviceIdType.MESH
TILE = 512
K = 256
KH = 128
RMAX = 64
F32 = jnp.float32
BF16 = jnp.bfloat16


def device(x, zl, k, y, zh):
    return (x * 8 + zl * 2 + k, y * 2 + zh)


def relay_source(z):
    return jnp.where(z == 4, 3, jnp.where(z == 3, 4, jnp.where(z == 6, 0, 7)))


def kernel(omega, psi, near, left, right, adm_in, ranks_in, y_out, z_out,
           om, ps, pr, nr, uu, vv, cr, cl, yp, y16, yr, yacc, yh, zp, zc, z16, zr,
           adm, ranks, load_sem, pr_send, pr_recv, ps_send, ps_recv, om_send, om_recv, tw_send, tw_recv,
           y_send, y_recv, h_send, h_recv, c_send, c_recv, z_send, z_recv):
    row = lax.axis_index("row")
    col = lax.axis_index("col")
    x, zl, k = row // 8, (row // 2) % 4, row % 2
    y, zh = col // 2, col % 2
    z = zh * 4 + zl
    place = row // 2

    xs, qs = y // 2, (y % 2) * 2 + zh
    ps_y = 2 * x + zl // 2
    tx = y // 2
    serves = (y % 2) == (zl // 2)
    holds = zh == zl % 2
    own_psi = serves & (x == tx)
    relayed = serves & jnp.logical_not(holds)
    rz = relay_source(z)
    tz = jnp.where(z == 3, 4, jnp.where(z == 4, 3, jnp.where(z == 0, 6, 1)))
    relays = jnp.where((z == 3) | (z == 7), y % 2 == 0, ((z == 4) | (z == 0)) & (y % 2 == 1))
    om_root = (x == xs) & (zl == qs)
    first = k == 0

    def remote(src, dst, ss, rs, dev):
        return pltpu.make_async_remote_copy(src_ref=src, dst_ref=dst, send_sem=ss, recv_sem=rs,
                                            device_id=dev, device_id_type=MESH)

    u, v = jnp.where(first, x, zl), jnp.where(first, zl, x)
    us, vs = jnp.where(first, xs, qs), jnp.where(first, qs, xs)
    on_axis = v == vs

    def at(a, b):
        return device(jnp.where(first, a, b), jnp.where(first, b, a), k, y, zh)

    barrier = pltpu.get_barrier_semaphore()

    def greet(dev):
        pl.semaphore_signal(barrier, inc=1, device_id=dev, device_id_type=MESH)

    count = 0
    for i in range(4):
        @pl.when(jnp.logical_not(own_psi & (x == i)))
        def _(i=i):
            greet(device(i, zl, k, ps_y, zh))

    @pl.when(relayed)
    def _():
        greet(device(x, rz % 4, k, y, rz // 4))
    count += jnp.where(relays, 1, 0) + jnp.where(serves, jnp.where(x == tx, 7, 8), 0)

    @pl.when(on_axis & (u != us))
    def _():
        greet(at(us, vs))

    @pl.when(jnp.logical_not(on_axis))
    def _():
        greet(at(u, vs))

    @pl.when(jnp.logical_not(om_root))
    def _():
        for i in range(1, 4):
            greet(at((u + i) % 4, v))
    count += jnp.where(om_root, 3, 0) + jnp.where(on_axis, 3, 0)
    count += jnp.where(on_axis & (u != us), 2, 3)
    greet(device(x, zl, 1 - k, y, zh))
    for i in range(1, 8):
        greet(device(x, zl, k, (y + i) % 8, zh))
    greet(device(x, zl, k, y, 1 - zh))
    for i in range(1, 16):
        p = (place + i) % 16
        greet(device(p // 4, p % 4, k, y, zh))
    count += 1 + 7 + 1 + 15

    loads = [pltpu.make_async_copy(right, vv, load_sem.at[0]),
             pltpu.make_async_copy(left, uu, load_sem.at[1]),
             pltpu.make_async_copy(near, nr, load_sem.at[2]),
             pltpu.make_async_copy(adm_in, adm, load_sem.at[3]),
             pltpu.make_async_copy(ranks_in, ranks, load_sem.at[4])]
    root_copies = [pltpu.make_async_copy(omega.at[:, pl.ds(h * KH, KH)], om.at[k, h], load_sem.at[5 + h])
                   for h in range(2)]

    @pl.when(om_root)
    def _():
        for c in root_copies:
            c.start()
    for c in loads:
        c.start()
    pl.semaphore_wait(barrier, count)

    @pl.when(om_root)
    def _():
        for c in root_copies:
            c.wait()

    sibling = device(x, zl, 1 - k, y, zh)
    my_quarter = pl.ds(pl.multiple_of(x * 256, 256), 256)
    pending = []

    def start(cond, c):
        pending.append((cond, c))
        if cond is None:
            c.start()
        else:
            @pl.when(cond)
            def _():
                c.start()

    def arrived(buf, sem):
        remote(buf, buf, c_send.at[0, 0], sem, sibling).wait_recv()

    def psi_part(h):
        return psi.at[pl.ds(pl.multiple_of(k * 1024 + x * 256, 256), 256), pl.ds(h * KH, KH)]

    def relay_psi(h):
        start(relays, remote(psi_part(h), pr.at[h], pr_send.at[h], pr_recv.at[h],
                             device(x, tz % 4, k, y, tz // 4)))

    def own_psi_copy(h, src):
        return pltpu.make_async_copy(src, ps.at[h, my_quarter], load_sem.at[7 + h])

    def send_psi(h, relay):
        cond = serves & (relayed if relay else holds)
        src = pr.at[h] if relay else psi_part(h)
        if relay:
            @pl.when(cond)
            def _():
                arrived(pr.at[h], pr_recv.at[h])
        for i in range(8):
            start(cond & jnp.logical_not((x == tx) & (y == i)),
                  remote(src, ps.at[h, my_quarter], ps_send.at[h, i], ps_recv.at[h, x], device(tx, zl, k, i, zh)))

        @pl.when(cond & (x == tx))
        def _():
            own_psi_copy(h, src).start()

    def psi_arrived(h):
        for i in range(4):
            @pl.when(jnp.logical_not(own_psi & (x == i)))
            def _(i=i):
                arrived(ps.at[h, pl.ds(i * 256, 256)], ps_recv.at[h, i])

        @pl.when(own_psi)
        def _():
            own_psi_copy(h, pr.at[h]).wait()

    def quarter(h, j):
        return om.at[k, h, pl.ds(pl.multiple_of(j * 256, 256), 256)]

    def send_omega(h, cond, j, sem, dev):
        start(cond, remote(quarter(h, j), quarter(h, j), om_send.at[h, sem], om_recv.at[h, j], dev))

    def scatter_omega(h):
        for i in range(1, 4):
            j = (us + i) % 4
            send_omega(h, om_root, j, i - 1, at(j, vs))

    def spread_omega(h):
        @pl.when(jnp.logical_not(om_root))
        def _():
            arrived(quarter(h, u), om_recv.at[h, u])
        for i in range(1, 4):
            send_omega(h, on_axis, u, 2 + i, at(u, (v + i) % 4))
        for i in range(1, 4):
            j = (u + i) % 4
            send_omega(h, jnp.logical_not(on_axis & (j == us)), u, 5 + i, at(j, v))

    def share_omega(h):
        for i in range(4):
            j = (u + i) % 4
            if i:
                @pl.when(jnp.logical_not(om_root))
                def _(j=j):
                    arrived(quarter(h, j), om_recv.at[h, j])
            start(None, remote(quarter(h, j), quarter(h, j), tw_send.at[h, j], tw_recv.at[h, j], sibling))

    def omega_arrived(h):
        for j in range(4):
            arrived(om.at[1 - k, h, pl.ds(256 * j, 256)], tw_recv.at[h, j])

    level = lax.broadcasted_iota(jnp.int32, (RMAX, KH), 0)

    def limit(a, b):
        return jnp.where(adm[a, b] == 1, ranks[a, b], 0)

    def flag(a, b):
        return jnp.where(adm[a, b] == 0, 1.0, 0.0).astype(F32)

    def dense(a, b, add):
        off = 4 * col + b - (2 * row + a) + 1

        @pl.when((off >= 0) & (off <= 2))
        def _():
            add(nr[a * TILE:(a + 1) * TILE, pl.ds(pl.multiple_of(off * TILE, TILE), TILE)])

    def left_products(h):
        for a in range(2):
            full = lax.dot_general(uu[a * TILE:(a + 1) * TILE, :], ps[h, a * TILE:(a + 1) * TILE, :],
                                   (((0,), (0,)), ((), ())), preferred_element_type=F32)
            for b in range(4):
                piece = full[b * RMAX:(b + 1) * RMAX]
                cl[b, a * RMAX:(a + 1) * RMAX, :] = jnp.where(level < limit(a, b), piece, 0.0).astype(BF16)
        for b in range(4):
            part = lax.dot_general(vv[:, b * TILE:(b + 1) * TILE], cl[b], (((0,), (0,)), ((), ())),
                                   preferred_element_type=F32)
            zp[h, 4 * b:4 * b + 4] = part.reshape(4, 2, 64, KH)
            for a in range(2):
                def add(block, a=a, b=b):
                    more = lax.dot_general(block, ps[h, a * TILE:(a + 1) * TILE, :], (((0,), (0,)), ((), ())),
                                           preferred_element_type=F32)
                    zp[h, 4 * b:4 * b + 4] += (more * flag(a, b)).reshape(4, 2, 64, KH)
                dense(a, b, add)
            start(None, remote(zp.at[h, pl.ds(4 * b, 4), 1 - k], zc.at[h, pl.ds(4 * b, 4)], c_send.at[h, b],
                               c_recv.at[h, b], sibling))

    def send_left(h):
        for b in range(4):
            arrived(zc.at[h, pl.ds(4 * b, 4)], c_recv.at[h, b])
            both = zc[h, 4 * b:4 * b + 4] + zp[h, 4 * b:4 * b + 4, k]
            zc[h, 4 * b:4 * b + 4] = both
            z16[h, 4 * b:4 * b + 4] = both.astype(BF16)
        for i in range(1, 16):
            p = (place + i) % 16
            start(None, remote(z16.at[h, p], zr.at[h, place], z_send.at[h, i], z_recv.at[h, place],
                               device(p // 4, p % 4, k, y, zh)))

    def sum_left(h):
        total = zc[h, place]
        for i in range(1, 16):
            p = (place + i) % 16
            arrived(zr.at[h, p], z_recv.at[h, p])
            total += zr[h, p].astype(F32)
        z_out[:, h * KH:(h + 1) * KH] = total

    def right_products(h):
        for b in range(4):
            full = jnp.dot(vv[:, b * TILE:(b + 1) * TILE], om[b // 2, h, (b % 2) * TILE:(b % 2 + 1) * TILE, :],
                           preferred_element_type=F32)
            for a in range(2):
                piece = full[a * RMAX:(a + 1) * RMAX]
                cr[a, b * RMAX:(b + 1) * RMAX, :] = jnp.where(level < limit(a, b), piece, 0.0).astype(BF16)
        for a in range(2):
            yp[h, 4 * a:4 * a + 4] = jnp.dot(uu[a * TILE:(a + 1) * TILE, :], cr[a],
                                             preferred_element_type=F32).reshape(4, 2, 64, KH)
            for b in range(4):
                def add(block, a=a, b=b):
                    more = jnp.dot(block, om[b // 2, h, (b % 2) * TILE:(b % 2 + 1) * TILE, :],
                                   preferred_element_type=F32)
                    yp[h, 4 * a:4 * a + 4] += (more * flag(a, b)).reshape(4, 2, 64, KH)
                dense(a, b, add)
            y16[h, 4 * a:4 * a + 4] = yp[h, 4 * a:4 * a + 4].astype(BF16)

    def send_right(h):
        for part in (1 - zh, zh):
            for i in range(1, 8):
                p = (y + i) % 8
                start(None, remote(y16.at[h, p, part], yr.at[h, y, part], y_send.at[h, part, i],
                                   y_recv.at[h, part, y], device(x, zl, k, p, zh)))

    def sum_right(h, part):
        total = yp[h, y, part]
        for i in range(1, 8):
            p = (y + i) % 8
            arrived(yr.at[h, p, part], y_recv.at[h, part, p])
            total += yr[h, p, part].astype(F32)
        return total

    def pass_right(h):
        yacc[h] = sum_right(h, 1 - zh)
        start(None, remote(yacc.at[h], yh.at[h], h_send.at[h], h_recv.at[h], device(x, zl, k, y, 1 - zh)))

    def end_right(h):
        total = sum_right(h, zh)
        arrived(yh.at[h], h_recv.at[h])
        y_out[:, h * KH:(h + 1) * KH] = total + yh[h]

    relay_psi(0)
    relay_psi(1)
    scatter_omega(0)
    send_psi(0, False)
    scatter_omega(1)
    send_psi(1, False)
    send_psi(0, True)
    spread_omega(0)
    send_psi(1, True)
    spread_omega(1)
    share_omega(0)
    for c in loads:
        c.wait()
    psi_arrived(0)
    left_products(0)
    omega_arrived(0)
    right_products(0)
    send_right(0)
    send_left(0)
    share_omega(1)
    psi_arrived(1)
    left_products(1)
    omega_arrived(1)
    right_products(1)
    send_right(1)
    send_left(1)
    pass_right(0)
    pass_right(1)
    sum_left(0)
    end_right(0)
    sum_left(1)
    end_right(1)

    for cond, c in pending:
        if cond is None:
            c.wait_send()
        else:
            @pl.when(cond)
            def _(c=c):
                c.wait_send()


def local(omega, psi, near_tiles, left_factors, right_factors, admissible, ranks):
    dma = pltpu.SemaphoreType.DMA
    anywhere = pl.BlockSpec(memory_space=pl.ANY)
    vmem = pl.BlockSpec(memory_space=pltpu.VMEM)
    out = jax.ShapeDtypeStruct((64, K), F32)
    return pl.pallas_call(
        kernel,
        out_shape=(out, out),
        in_specs=[anywhere] * 7,
        out_specs=(vmem, vmem),
        scratch_shapes=[
            pltpu.VMEM((2, 2, 1024, KH), BF16),
            pltpu.VMEM((2, 1024, KH), BF16),
            pltpu.VMEM((2, 256, KH), BF16),
            pltpu.VMEM((1024, 3 * TILE), BF16),
            pltpu.VMEM((1024, 256), BF16),
            pltpu.VMEM((128, 2048), BF16),
            pltpu.VMEM((2, 256, KH), BF16),
            pltpu.VMEM((4, 128, KH), BF16),
            pltpu.VMEM((2, 8, 2, 64, KH), F32),
            pltpu.VMEM((2, 8, 2, 64, KH), BF16),
            pltpu.VMEM((2, 8, 2, 64, KH), BF16),
            pltpu.VMEM((2, 64, KH), F32),
            pltpu.VMEM((2, 64, KH), F32),
            pltpu.VMEM((2, 16, 2, 64, KH), F32),
            pltpu.VMEM((2, 16, 64, KH), F32),
            pltpu.VMEM((2, 16, 64, KH), BF16),
            pltpu.VMEM((2, 16, 64, KH), BF16),
            pltpu.SMEM((2, 4), jnp.int32),
            pltpu.SMEM((2, 4), jnp.int32),
            dma((9,)), dma((2,)), dma((2,)), dma((2, 8)), dma((2, 4)), dma((2, 9)), dma((2, 4)), dma((2, 4)), dma((2, 4)),
            dma((2, 2, 8)), dma((2, 2, 8)), dma((2,)), dma((2,)), dma((2, 4)), dma((2, 4)),
            dma((2, 16)), dma((2, 16)),
        ],
        compiler_params=pltpu.CompilerParams(collective_id=0, has_side_effects=True,
                                             vmem_limit_bytes=64 << 20),
        cost_estimate=pl.CostEstimate(flops=2 * 10 ** 9, bytes_accessed=6 << 20, transcendentals=0),
    )(omega, psi, near_tiles, left_factors, right_factors, admissible, ranks)


def solution(mesh):
    return jax.shard_map(
        local,
        mesh=mesh,
        in_specs=(
            P("row", None),
            P("col", None),
            P("row", None),
            P("row", "col"),
            P("row", "col"),
            P("row", "col"),
            P("row", "col"),
        ),
        out_specs=(P(("row", "col"), None), P(("col", "row"), None)),
        check_vma=False,
    )
```

```python
import jax
import jax.numpy as jnp
from jax import lax
from jax.experimental import pallas as pl
from jax.experimental.pallas import tpu as pltpu
from jax.sharding import PartitionSpec as P

MESH = pl.DeviceIdType.MESH
TILE = 512
K = 256
KH = 128
RMAX = 64
F32 = jnp.float32
BF16 = jnp.bfloat16


def device(x, zl, k, y, zh):
    return (x * 8 + zl * 2 + k, y * 2 + zh)


def relay_source(z):
    return jnp.where(z == 4, 3, jnp.where(z == 3, 4, jnp.where(z == 6, 0, 7)))


def kernel(omega, psi, near, left, right, adm_in, ranks_in, r_out,
           om, ps, pr, rb, nr, uu, vv, cr, cl, yp, y16, yr, yacc, yh, zp, zc, z16, zr,
           adm, ranks, load_sem, pr_send, pr_recv, rb_send, rb_recv, ps_send, ps_recv, om_send, om_recv, tw_send, tw_recv,
           y_send, y_recv, h_send, h_recv, c_send, c_recv, z_send, z_recv):
    row = lax.axis_index("row")
    col = lax.axis_index("col")
    x, zl, k = row // 8, (row // 2) % 4, row % 2
    y, zh = col // 2, col % 2
    z = zh * 4 + zl
    place = row // 2

    xs, qs = y // 2, (y % 2) * 2 + zh
    ps_y = 2 * x + zl // 2
    tx = y // 2
    dist = (y - ps_y + 8) % 8
    serves = (y % 2) == (zl // 2)
    holds = zh == zl % 2
    own_psi = serves & (dist != 4)
    relayed = serves & jnp.logical_not(holds)
    rz = relay_source(z)
    tz = jnp.where(z == 3, 4, jnp.where(z == 4, 3, jnp.where(z == 0, 6, 1)))
    relays = jnp.where((z == 3) | (z == 7), y % 2 == 0, ((z == 4) | (z == 0)) & (y % 2 == 1))
    steps = (2, 6)
    passed = [((y + 8 - g) % 8) // 2 for g in steps]
    om_root = (x == xs) & (zl == qs)
    first = k == 0

    def remote(src, dst, ss, rs, dev):
        return pltpu.make_async_remote_copy(src_ref=src, dst_ref=dst, send_sem=ss, recv_sem=rs,
                                            device_id=dev, device_id_type=MESH)

    u, v = jnp.where(first, x, zl), jnp.where(first, zl, x)
    us, vs = jnp.where(first, xs, qs), jnp.where(first, qs, xs)
    on_axis = v == vs

    def at(a, b):
        return device(jnp.where(first, a, b), jnp.where(first, b, a), k, y, zh)

    barrier = pltpu.get_barrier_semaphore()

    def greet(dev):
        pl.semaphore_signal(barrier, inc=1, device_id=dev, device_id_type=MESH)

    count = 0
    near_by = (dist <= 1) | (dist == 7)
    for i in range(4):
        remote_part = jnp.logical_not(own_psi & (x == i))

        @pl.when(remote_part & near_by)
        def _(i=i):
            greet(device(i, zl, k, ps_y, zh))

        @pl.when(remote_part & (dist >= 2) & (dist <= 4))
        def _(i=i):
            greet(device(i, zl, k, (ps_y + 2) % 8, zh))

        @pl.when(remote_part & (dist >= 4) & (dist <= 6))
        def _(i=i):
            greet(device(i, zl, k, (ps_y + 6) % 8, zh))

    @pl.when(serves)
    def _():
        for g in steps:
            greet(device(x, zl, k, (y + g) % 8, zh))

    @pl.when(relayed)
    def _():
        greet(device(x, rz % 4, k, y, rz // 4))
    count += jnp.where(relays, 1, 0) + jnp.where(serves, 11, 0)
    for target in [tx] + passed:
        count -= jnp.where(serves & (x == target), 1, 0)

    @pl.when(on_axis & (u != us))
    def _():
        greet(at(us, vs))

    @pl.when(jnp.logical_not(on_axis))
    def _():
        greet(at(u, vs))

    @pl.when(jnp.logical_not(om_root))
    def _():
        for i in range(1, 4):
            greet(at((u + i) % 4, v))
    count += jnp.where(om_root, 3, 0) + jnp.where(on_axis, 3, 0)
    count += jnp.where(on_axis & (u != us), 2, 3)
    greet(device(x, zl, 1 - k, y, zh))
    for i in range(1, 8):
        greet(device(x, zl, k, (y + i) % 8, zh))
    greet(device(x, zl, k, y, 1 - zh))
    for i in range(1, 16):
        p = (place + i) % 16
        greet(device(p // 4, p % 4, k, y, zh))
    count += 1 + 7 + 1 + 15

    loads = [pltpu.make_async_copy(right, vv, load_sem.at[0]),
             pltpu.make_async_copy(left, uu, load_sem.at[1]),
             pltpu.make_async_copy(near, nr, load_sem.at[2]),
             pltpu.make_async_copy(adm_in, adm, load_sem.at[3]),
             pltpu.make_async_copy(ranks_in, ranks, load_sem.at[4])]
    root_copies = [pltpu.make_async_copy(omega.at[:, pl.ds(h * KH, KH)], om.at[k, h], load_sem.at[5 + h])
                   for h in range(2)]

    @pl.when(om_root)
    def _():
        for c in root_copies:
            c.start()
    for c in loads:
        c.start()
    pl.semaphore_wait(barrier, count)

    @pl.when(om_root)
    def _():
        for c in root_copies:
            c.wait()

    sibling = device(x, zl, 1 - k, y, zh)
    my_quarter = pl.ds(pl.multiple_of(x * 256, 256), 256)
    pending = []

    def start(cond, c):
        pending.append((cond, c))
        if cond is None:
            c.start()
        else:
            @pl.when(cond)
            def _():
                c.start()

    def flush():
        for cond, c in pending:
            if cond is None:
                c.wait_send()
            else:
                @pl.when(cond)
                def _(c=c):
                    c.wait_send()
        pending.clear()

    def arrived(buf, sem):
        remote(buf, buf, c_send.at[0, 0], sem, sibling).wait_recv()

    def psi_part(h):
        return psi.at[pl.ds(pl.multiple_of(k * 1024 + x * 256, 256), 256), pl.ds(h * KH, KH)]

    def relay_psi(h):
        start(relays, remote(psi_part(h), pr.at[h], pr_send.at[h], pr_recv.at[h],
                             device(x, tz % 4, k, y, tz // 4)))

    def own_psi_copy(h, src):
        return pltpu.make_async_copy(src, ps.at[h, my_quarter], load_sem.at[7 + h])

    def psi_final(h, cond, src, target, there, sem, rows=None):
        dst = my_quarter
        if rows is not None:
            src = src.at[pl.ds(rows, 128)]
            dst = pl.ds(pl.multiple_of(x * 256 + rows, 128), 128)
        start(cond, remote(src, ps.at[h, dst], ps_send.at[h, sem], ps_recv.at[h, x], device(target, zl, k, there, zh)))

    def send_psi(h, relay):
        cond = serves & (relayed if relay else holds)
        src = pr.at[h] if relay else psi_part(h)
        if relay:
            @pl.when(cond)
            def _():
                arrived(pr.at[h], pr_recv.at[h])
        for n, g in enumerate(steps):
            start(cond, remote(src, rb.at[h, n], rb_send.at[h, n], rb_recv.at[h, n],
                               device(x, zl, k, (y + g) % 8, zh)))
        psi_final(h, cond, src, tx, (y + 1) % 8, 0)
        psi_final(h, cond, src, tx, (y + 7) % 8, 1)
        psi_final(h, cond & (x != tx), src, tx, y, 2)

        @pl.when(cond & (x == tx))
        def _():
            own_psi_copy(h, src).start()

    def pass_psi(h, relay):
        cond = serves & (relayed if relay else holds)
        for n, g in enumerate(steps):
            @pl.when(cond)
            def _(n=n):
                arrived(rb.at[h, n], rb_recv.at[h, n])
            src, to, way = rb.at[h, n], passed[n], (1, 7)[n]
            psi_final(h, cond, src, to, (y + way) % 8, 3 + 3 * n)
            psi_final(h, cond, src, to, (y + 2 * way) % 8, 4 + 3 * n, 128 * n)
            psi_final(h, cond & (x != to), src, to, y, 5 + 3 * n)

            @pl.when(cond & (x == to))
            def _(src=src):
                own_psi_copy(h, src).start()

    def psi_arrived(h):
        for i in range(4):
            @pl.when(jnp.logical_not(own_psi & (x == i)))
            def _(i=i):
                arrived(ps.at[h, pl.ds(i * 256, 256)], ps_recv.at[h, i])

        @pl.when(own_psi)
        def _():
            own_psi_copy(h, pr.at[h]).wait()

    def quarter(h, j):
        return om.at[k, h, pl.ds(pl.multiple_of(j * 256, 256), 256)]

    def send_omega(h, cond, j, sem, dev):
        start(cond, remote(quarter(h, j), quarter(h, j), om_send.at[h, sem], om_recv.at[h, j], dev))

    def scatter_omega(h):
        for i in range(1, 4):
            j = (us + i) % 4
            send_omega(h, om_root, j, i - 1, at(j, vs))

    def spread_omega(h):
        @pl.when(jnp.logical_not(om_root))
        def _():
            arrived(quarter(h, u), om_recv.at[h, u])
        for i in range(1, 4):
            send_omega(h, on_axis, u, 2 + i, at(u, (v + i) % 4))
        for i in range(1, 4):
            j = (u + i) % 4
            send_omega(h, jnp.logical_not(on_axis & (j == us)), u, 5 + i, at(j, v))

    def share_omega(h):
        for i in range(4):
            j = (u + i) % 4
            if i:
                @pl.when(jnp.logical_not(om_root))
                def _(j=j):
                    arrived(quarter(h, j), om_recv.at[h, j])
            start(None, remote(quarter(h, j), quarter(h, j), tw_send.at[h, j], tw_recv.at[h, j], sibling))

    def omega_arrived(h):
        for j in range(4):
            arrived(om.at[1 - k, h, pl.ds(256 * j, 256)], tw_recv.at[h, j])

    level = lax.broadcasted_iota(jnp.int32, (RMAX, KH), 0)

    def limit(a, b):
        return jnp.where(adm[a, b] == 1, ranks[a, b], 0)

    def flag(a, b):
        return jnp.where(adm[a, b] == 0, 1.0, 0.0).astype(F32)

    def dense(a, b, add):
        off = 4 * col + b - (2 * row + a) + 1

        @pl.when((off >= 0) & (off <= 2))
        def _():
            add(nr[a * TILE:(a + 1) * TILE, pl.ds(pl.multiple_of(off * TILE, TILE), TILE)])

    def left_products(h):
        for a in range(2):
            full = lax.dot_general(uu[a * TILE:(a + 1) * TILE, :], ps[h, a * TILE:(a + 1) * TILE, :],
                                   (((0,), (0,)), ((), ())), preferred_element_type=F32)
            for b in range(4):
                piece = full[b * RMAX:(b + 1) * RMAX]
                cl[b, a * RMAX:(a + 1) * RMAX, :] = jnp.where(level < limit(a, b), piece, 0.0).astype(BF16)
        for b in range(4):
            part = lax.dot_general(vv[:, b * TILE:(b + 1) * TILE], cl[b], (((0,), (0,)), ((), ())),
                                   preferred_element_type=F32)
            zp[h, 4 * b:4 * b + 4] = part.reshape(4, 2, 64, KH)
            for a in range(2):
                def add(block, a=a, b=b):
                    more = lax.dot_general(block, ps[h, a * TILE:(a + 1) * TILE, :], (((0,), (0,)), ((), ())),
                                           preferred_element_type=F32)
                    zp[h, 4 * b:4 * b + 4] += (more * flag(a, b)).reshape(4, 2, 64, KH)
                dense(a, b, add)
            start(None, remote(zp.at[h, pl.ds(4 * b, 4), 1 - k], zc.at[h, pl.ds(4 * b, 4)], c_send.at[h, b],
                               c_recv.at[h, b], sibling))

    def send_left(h):
        for b in range(4):
            arrived(zc.at[h, pl.ds(4 * b, 4)], c_recv.at[h, b])
            both = zc[h, 4 * b:4 * b + 4] + zp[h, 4 * b:4 * b + 4, k]
            zc[h, 4 * b:4 * b + 4] = both
            z16[h, 4 * b:4 * b + 4] = both.astype(BF16)
        for i in range(1, 16):
            p = (place + i) % 16
            start(None, remote(z16.at[h, p], zr.at[h, place], z_send.at[h, i], z_recv.at[h, place],
                               device(p // 4, p % 4, k, y, zh)))

    def sum_left(h):
        for i in range(1, 16):
            p = (place + i) % 16
            arrived(zr.at[h, p], z_recv.at[h, p])
            more = zr[h, p].astype(F32)
            total = more if i == 1 else total + more
        r_out[2, :, h * KH:(h + 1) * KH] = total
        r_out[3, :, h * KH:(h + 1) * KH] = zc[h, place]

    def right_products(h):
        for b in range(4):
            full = jnp.dot(vv[:, b * TILE:(b + 1) * TILE], om[b // 2, h, (b % 2) * TILE:(b % 2 + 1) * TILE, :],
                           preferred_element_type=F32)
            for a in range(2):
                piece = full[a * RMAX:(a + 1) * RMAX]
                cr[a, b * RMAX:(b + 1) * RMAX, :] = jnp.where(level < limit(a, b), piece, 0.0).astype(BF16)
        for a in range(2):
            yp[h, 4 * a:4 * a + 4] = jnp.dot(uu[a * TILE:(a + 1) * TILE, :], cr[a],
                                             preferred_element_type=F32).reshape(4, 2, 64, KH)
            for b in range(4):
                def add(block, a=a, b=b):
                    more = jnp.dot(block, om[b // 2, h, (b % 2) * TILE:(b % 2 + 1) * TILE, :],
                                   preferred_element_type=F32)
                    yp[h, 4 * a:4 * a + 4] += (more * flag(a, b)).reshape(4, 2, 64, KH)
                dense(a, b, add)
            y16[h, 4 * a:4 * a + 4] = yp[h, 4 * a:4 * a + 4].astype(BF16)

    def send_right(h):
        for part in (1 - zh, zh):
            for i in range(1, 8):
                p = (y + i) % 8
                start(None, remote(y16.at[h, p, part], yr.at[h, y, part], y_send.at[h, part, i],
                                   y_recv.at[h, part, y], device(x, zl, k, p, zh)))

    def sum_right(h, part):
        total = yp[h, y, part]
        for i in range(1, 8):
            p = (y + i) % 8
            arrived(yr.at[h, p, part], y_recv.at[h, part, p])
            total += yr[h, p, part].astype(F32)
        return total

    def pass_right(h):
        yacc[h] = sum_right(h, 1 - zh)
        start(None, remote(yacc.at[h], yh.at[h], h_send.at[h], h_recv.at[h], device(x, zl, k, y, 1 - zh)))

    def end_right(h):
        total = sum_right(h, zh)
        arrived(yh.at[h], h_recv.at[h])
        r_out[0, :, h * KH:(h + 1) * KH] = total
        r_out[1, :, h * KH:(h + 1) * KH] = yh[h]

    relay_psi(0)
    relay_psi(1)
    scatter_omega(0)
    send_psi(0, False)
    scatter_omega(1)
    send_psi(1, False)
    send_psi(0, True)
    send_psi(1, True)
    pass_psi(0, False)
    pass_psi(1, False)
    spread_omega(0)
    pass_psi(0, True)
    spread_omega(1)
    pass_psi(1, True)
    share_omega(0)
    for c in loads:
        c.wait()
    psi_arrived(0)
    left_products(0)
    omega_arrived(0)
    right_products(0)
    send_right(0)
    send_left(0)
    share_omega(1)
    psi_arrived(1)
    left_products(1)
    omega_arrived(1)
    right_products(1)
    send_right(1)
    rest = pending[:]
    send_left(1)
    late = pending[len(rest):]
    pending[:] = rest
    flush()
    pending[:] = late
    pass_right(0)
    pass_right(1)
    last = pending[-2:]
    del pending[-2:]
    sum_left(0)
    flush()
    pending[:] = last
    sum_left(1)
    end_right(0)
    end_right(1)

    flush()


def local(omega, psi, near_tiles, left_factors, right_factors, admissible, ranks):
    dma = pltpu.SemaphoreType.DMA
    anywhere = pl.BlockSpec(memory_space=pl.ANY)
    vmem = pl.BlockSpec(memory_space=pltpu.VMEM)
    out = jax.ShapeDtypeStruct((4, 64, K), F32)
    parts = pl.pallas_call(
        kernel,
        out_shape=out,
        in_specs=[anywhere] * 7,
        out_specs=vmem,
        scratch_shapes=[
            pltpu.VMEM((2, 2, 1024, KH), BF16),
            pltpu.VMEM((2, 1024, KH), BF16),
            pltpu.VMEM((2, 256, KH), BF16),
            pltpu.VMEM((2, 2, 256, KH), BF16),
            pltpu.VMEM((1024, 3 * TILE), BF16),
            pltpu.VMEM((1024, 256), BF16),
            pltpu.VMEM((128, 2048), BF16),
            pltpu.VMEM((2, 256, KH), BF16),
            pltpu.VMEM((4, 128, KH), BF16),
            pltpu.VMEM((2, 8, 2, 64, KH), F32),
            pltpu.VMEM((2, 8, 2, 64, KH), BF16),
            pltpu.VMEM((2, 8, 2, 64, KH), BF16),
            pltpu.VMEM((2, 64, KH), F32),
            pltpu.VMEM((2, 64, KH), F32),
            pltpu.VMEM((2, 16, 2, 64, KH), F32),
            pltpu.VMEM((2, 16, 64, KH), F32),
            pltpu.VMEM((2, 16, 64, KH), BF16),
            pltpu.VMEM((2, 16, 64, KH), BF16),
            pltpu.SMEM((2, 4), jnp.int32),
            pltpu.SMEM((2, 4), jnp.int32),
            dma((9,)), dma((2,)), dma((2,)), dma((2, 2)), dma((2, 2)), dma((2, 9)), dma((2, 4)), dma((2, 9)), dma((2, 4)), dma((2, 4)), dma((2, 4)),
            dma((2, 2, 8)), dma((2, 2, 8)), dma((2,)), dma((2,)), dma((2, 4)), dma((2, 4)),
            dma((2, 16)), dma((2, 16)),
        ],
        compiler_params=pltpu.CompilerParams(collective_id=0, has_side_effects=True,
                                             vmem_limit_bytes=64 << 20),
        cost_estimate=pl.CostEstimate(flops=2 * 10 ** 9, bytes_accessed=6 << 20, transcendentals=0),
    )(omega, psi, near_tiles, left_factors, right_factors, admissible, ranks)
    return (parts[0] + parts[1], parts[2] + parts[3])


def solution(mesh):
    return jax.shard_map(
        local,
        mesh=mesh,
        in_specs=(
            P("row", None),
            P("col", None),
            P("row", None),
            P("row", "col"),
            P("row", "col"),
            P("row", "col"),
            P("row", "col"),
        ),
        out_specs=(P(("row", "col"), None), P(("col", "row"), None)),
        check_vma=False,
    )
```

```python
import jax
import jax.numpy as jnp
from jax import lax
from jax.experimental import pallas as pl
from jax.experimental.pallas import tpu as pltpu
from jax.sharding import PartitionSpec as P

MESH = pl.DeviceIdType.MESH
TILE = 512
K = 256
KH = 128
RMAX = 64
F32 = jnp.float32
BF16 = jnp.bfloat16


def device(x, zl, k, y, zh):
    return (x * 8 + zl * 2 + k, y * 2 + zh)


def relay_source(z):
    return jnp.where(z == 4, 3, jnp.where(z == 3, 4, jnp.where(z == 6, 0, 7)))


def kernel(omega, psi, near, left, right, adm_in, ranks_in, r_out,
           om, ps, pq, pr, rb, nr, uu, vv, cr, cl, yp, y16, yr, yacc, yh, zp, zc, z16, zr,
           adm, ranks, load_sem, pr_send, pr_recv, rb_send, rb_recv, ps_send, ps_recv, om_send, om_recv, tw_send, tw_recv,
           y_send, y_recv, h_send, h_recv, c_send, c_recv, z_send, z_recv):
    row = lax.axis_index("row")
    col = lax.axis_index("col")
    x, zl, k = row // 8, (row // 2) % 4, row % 2
    y, zh = col // 2, col % 2
    z = zh * 4 + zl
    place = row // 2

    xs, qs = y // 2, (y % 2) * 2 + zh
    ps_y = 2 * x + zl // 2
    tx = y // 2
    dist = (y - ps_y + 8) % 8
    serves = (y % 2) == (zl // 2)
    holds = zh == zl % 2
    own_psi = serves & (dist != 4)
    relayed = serves & jnp.logical_not(holds)
    rz = relay_source(z)
    tz = jnp.where(z == 3, 4, jnp.where(z == 4, 3, jnp.where(z == 0, 6, 1)))
    relays = jnp.where((z == 3) | (z == 7), y % 2 == 0, ((z == 4) | (z == 0)) & (y % 2 == 1))
    steps = (2, 6)
    passed = [((y + 8 - g) % 8) // 2 for g in steps]
    om_root = (x == xs) & (zl == qs)
    first = k == 0

    def remote(src, dst, ss, rs, dev):
        return pltpu.make_async_remote_copy(src_ref=src, dst_ref=dst, send_sem=ss, recv_sem=rs,
                                            device_id=dev, device_id_type=MESH)

    u, v = jnp.where(first, x, zl), jnp.where(first, zl, x)
    us, vs = jnp.where(first, xs, qs), jnp.where(first, qs, xs)
    on_axis = v == vs

    def at(a, b):
        return device(jnp.where(first, a, b), jnp.where(first, b, a), k, y, zh)

    barrier = pltpu.get_barrier_semaphore()

    def greet(dev):
        pl.semaphore_signal(barrier, inc=1, device_id=dev, device_id_type=MESH)

    count = 0
    near_by = (dist <= 1) | (dist == 7)
    for i in range(4):
        remote_part = jnp.logical_not(own_psi & (x == i))

        @pl.when(remote_part & near_by)
        def _(i=i):
            greet(device(i, zl, k, ps_y, zh))

        @pl.when(remote_part & (dist >= 2) & (dist <= 4))
        def _(i=i):
            greet(device(i, zl, k, (ps_y + 2) % 8, zh))

        @pl.when(remote_part & (dist >= 4) & (dist <= 6))
        def _(i=i):
            greet(device(i, zl, k, (ps_y + 6) % 8, zh))

    @pl.when(serves)
    def _():
        for g in steps:
            greet(device(x, zl, k, (y + g) % 8, zh))

    @pl.when(relayed)
    def _():
        greet(device(x, rz % 4, k, y, rz // 4))
    count += jnp.where(relays, 1, 0) + jnp.where(serves, 11, 0)
    for target in [tx] + passed:
        count -= jnp.where(serves & (x == target), 1, 0)

    @pl.when(on_axis & (u != us))
    def _():
        greet(at(us, vs))

    @pl.when(jnp.logical_not(on_axis))
    def _():
        greet(at(u, vs))

    @pl.when(jnp.logical_not(om_root))
    def _():
        for i in range(1, 4):
            greet(at((u + i) % 4, v))
    count += jnp.where(om_root, 3, 0) + jnp.where(on_axis, 3, 0)
    count += jnp.where(on_axis & (u != us), 2, 3)
    greet(device(x, zl, 1 - k, y, zh))
    for i in range(1, 8):
        greet(device(x, zl, k, (y + i) % 8, zh))
    greet(device(x, zl, k, y, 1 - zh))
    for i in range(1, 16):
        p = (place + i) % 16
        greet(device(p // 4, p % 4, k, y, zh))
    count += 1 + 7 + 1 + 15

    loads = [pltpu.make_async_copy(right, vv, load_sem.at[0]),
             pltpu.make_async_copy(left, uu, load_sem.at[1]),
             pltpu.make_async_copy(near, nr, load_sem.at[2]),
             pltpu.make_async_copy(adm_in, adm, load_sem.at[3]),
             pltpu.make_async_copy(ranks_in, ranks, load_sem.at[4])]
    root_copies = [pltpu.make_async_copy(omega.at[:, pl.ds(h * KH, KH)], om.at[k, h], load_sem.at[5 + h])
                   for h in range(2)]

    @pl.when(om_root)
    def _():
        for c in root_copies:
            c.start()
    for c in loads:
        c.start()
    root_psi = [pltpu.make_async_copy(psi.at[pl.ds(pl.multiple_of(k * 1024, 1024), 1024), pl.ds(h * KH, KH)], pq.at[h],
                                      load_sem.at[9 + h]) for h in range(2)]

    @pl.when(om_root)
    def _():
        for c in root_psi:
            c.start()
    yp[...] = jnp.zeros_like(yp)
    zp[...] = jnp.zeros_like(zp)
    pl.semaphore_wait(barrier, count)

    @pl.when(om_root)
    def _():
        for c in root_copies:
            c.wait()

    sibling = device(x, zl, 1 - k, y, zh)
    my_quarter = pl.ds(pl.multiple_of(x * 256, 256), 256)
    pending = []

    def start(cond, c):
        pending.append((cond, c))
        if cond is None:
            c.start()
        else:
            @pl.when(cond)
            def _():
                c.start()

    def flush():
        for cond, c in pending:
            if cond is None:
                c.wait_send()
            else:
                @pl.when(cond)
                def _(c=c):
                    c.wait_send()
        pending.clear()

    def arrived(buf, sem):
        remote(buf, buf, c_send.at[0, 0], sem, sibling).wait_recv()

    def psi_part(h):
        return psi.at[pl.ds(pl.multiple_of(k * 1024 + x * 256, 256), 256), pl.ds(h * KH, KH)]

    def relay_psi(h):
        start(relays, remote(psi_part(h), pr.at[h], pr_send.at[h], pr_recv.at[h],
                             device(x, tz % 4, k, y, tz // 4)))

    def own_psi_copy(h, src):
        return pltpu.make_async_copy(src, ps.at[h, my_quarter], load_sem.at[7 + h])

    def psi_final(h, cond, src, target, there, sem, rows=None):
        dst = my_quarter
        if rows is not None:
            src = src.at[pl.ds(rows, 128)]
            dst = pl.ds(pl.multiple_of(x * 256 + rows, 128), 128)
        start(cond, remote(src, ps.at[h, dst], ps_send.at[h, sem], ps_recv.at[h, x], device(target, zl, k, there, zh)))

    def send_psi(h, relay):
        cond = serves & (relayed if relay else holds)
        src = pr.at[h] if relay else psi_part(h)
        if relay:
            @pl.when(cond)
            def _():
                arrived(pr.at[h], pr_recv.at[h])
        for n, g in enumerate(steps):
            start(cond, remote(src, rb.at[h, n], rb_send.at[h, n], rb_recv.at[h, n],
                               device(x, zl, k, (y + g) % 8, zh)))
        psi_final(h, cond, src, tx, (y + 1) % 8, 0)
        psi_final(h, cond, src, tx, (y + 7) % 8, 1)
        psi_final(h, cond & (x != tx), src, tx, y, 2)

        @pl.when(cond & (x == tx))
        def _():
            own_psi_copy(h, src).start()

    def pass_psi(h, relay):
        cond = serves & (relayed if relay else holds)
        for n, g in enumerate(steps):
            @pl.when(cond)
            def _(n=n):
                arrived(rb.at[h, n], rb_recv.at[h, n])
            src, to, way = rb.at[h, n], passed[n], (1, 7)[n]
            psi_final(h, cond, src, to, (y + way) % 8, 3 + 3 * n)
            psi_final(h, cond, src, to, (y + 2 * way) % 8, 4 + 3 * n, 128 * n)
            psi_final(h, cond & (x != to), src, to, y, 5 + 3 * n)

            @pl.when(cond & (x == to))
            def _(src=src):
                own_psi_copy(h, src).start()

    def psi_arrived(h):
        for i in range(4):
            @pl.when(jnp.logical_not(own_psi & (x == i)))
            def _(i=i):
                arrived(ps.at[h, pl.ds(i * 256, 256)], ps_recv.at[h, i])

        @pl.when(own_psi)
        def _():
            own_psi_copy(h, pr.at[h]).wait()

    def quarter(h, j):
        return om.at[k, h, pl.ds(pl.multiple_of(j * 256, 256), 256)]

    def send_omega(h, cond, j, sem, dev):
        start(cond, remote(quarter(h, j), quarter(h, j), om_send.at[h, sem], om_recv.at[h, j], dev))

    def scatter_omega(h):
        for i in range(1, 4):
            j = (us + i) % 4
            send_omega(h, om_root, j, i - 1, at(j, vs))

    def spread_omega(h, along):
        cond = on_axis if along else jnp.logical_not(on_axis)

        @pl.when(cond & jnp.logical_not(om_root))
        def _():
            arrived(quarter(h, u), om_recv.at[h, u])
        if along:
            for i in range(1, 4):
                send_omega(h, on_axis, u, 2 + i, at(u, (v + i) % 4))
        for i in range(1, 4):
            j = (u + i) % 4
            send_omega(h, cond & (j != us) if along else cond, u, 5 + i, at(j, v))
        start(cond & jnp.logical_not(om_root),
              remote(quarter(h, u), quarter(h, u), tw_send.at[h, 0], tw_recv.at[h, u], sibling))

    def share_omega(h):
        for i in range(1, 4):
            j = (u + i) % 4

            @pl.when(jnp.logical_not(om_root))
            def _(j=j):
                arrived(quarter(h, j), om_recv.at[h, j])
            start(jnp.logical_not(om_root),
                  remote(quarter(h, j), quarter(h, j), tw_send.at[h, i], tw_recv.at[h, j], sibling))

    def omega_arrived(h):
        @pl.when(jnp.logical_not(om_root))
        def _():
            for j in range(4):
                arrived(om.at[1 - k, h, pl.ds(256 * j, 256)], tw_recv.at[h, j])

    level = lax.broadcasted_iota(jnp.int32, (RMAX, KH), 0)

    def limit(a, b):
        return jnp.where(adm[a, b] == 1, ranks[a, b], 0)

    def flag(a, b):
        return jnp.where(adm[a, b] == 0, 1.0, 0.0).astype(F32)

    corners = {(0, 3): row == 2 * col + 2, (1, 0): row == 2 * col - 1}

    def tile(a, off):
        return nr[a * TILE:(a + 1) * TILE, pl.ds(pl.multiple_of(off * TILE, TILE), TILE)]

    def add_right(h, a, b, block):
        more = jnp.dot(block, om[b // 2, h, (b % 2) * TILE:(b % 2 + 1) * TILE, :], preferred_element_type=F32)
        yp[h, 4 * a:4 * a + 4] += (more * flag(a, b)).reshape(4, 2, 64, KH)

    def add_left(h, a, b, block, rows):
        more = lax.dot_general(block, rows[h, a * TILE:(a + 1) * TILE, :], (((0,), (0,)), ((), ())),
                               preferred_element_type=F32)
        zp[h, 4 * b:4 * b + 4] += (more * flag(a, b)).reshape(4, 2, 64, KH)

    def share_root():
        for h in range(2):
            start(om_root, remote(om.at[k, h], om.at[k, h], tw_send.at[h, 0], tw_recv.at[h, 0], sibling))

    def diagonal_products():
        @pl.when(om_root)
        def _():
            for c in root_psi:
                c.wait()
            for h in range(2):
                arrived(om.at[1 - k, h], tw_recv.at[h, 0])
            for a in range(2):
                for b in range(4):
                    off = b - 2 * k - a + 1

                    @pl.when((off >= 0) & (off <= 2))
                    def _(a=a, b=b, off=off):
                        for h in range(2):
                            add_right(h, a, b, tile(a, off))
                            add_left(h, a, b, tile(a, off), pq)

    def left_products(h):
        for a in range(2):
            full = lax.dot_general(uu[a * TILE:(a + 1) * TILE, :], ps[h, a * TILE:(a + 1) * TILE, :],
                                   (((0,), (0,)), ((), ())), preferred_element_type=F32)
            for b in range(4):
                piece = full[b * RMAX:(b + 1) * RMAX]
                cl[b, a * RMAX:(a + 1) * RMAX, :] = jnp.where(level < limit(a, b), piece, 0.0).astype(BF16)
        for b in range(4):
            part = lax.dot_general(vv[:, b * TILE:(b + 1) * TILE], cl[b], (((0,), (0,)), ((), ())),
                                   preferred_element_type=F32)
            zp[h, 4 * b:4 * b + 4] += part.reshape(4, 2, 64, KH)
            for a, corner, off in ((0, 3, 0), (1, 0, 2)):
                if b == corner:
                    @pl.when(corners[a, b])
                    def _(a=a, b=b, off=off):
                        add_left(h, a, b, tile(a, off), ps)
            start(None, remote(zp.at[h, pl.ds(4 * b, 4), 1 - k], zc.at[h, pl.ds(4 * b, 4)], c_send.at[h, b],
                               c_recv.at[h, b], sibling))

    def send_left(h):
        for b in range(4):
            arrived(zc.at[h, pl.ds(4 * b, 4)], c_recv.at[h, b])
            both = zc[h, 4 * b:4 * b + 4] + zp[h, 4 * b:4 * b + 4, k]
            zc[h, 4 * b:4 * b + 4] = both
            z16[h, 4 * b:4 * b + 4] = both.astype(BF16)
        for i in range(1, 16):
            p = (place + i) % 16
            start(None, remote(z16.at[h, p], zr.at[h, place], z_send.at[h, i], z_recv.at[h, place],
                               device(p // 4, p % 4, k, y, zh)))

    def sum_left(h):
        for i in range(1, 16):
            p = (place + i) % 16
            arrived(zr.at[h, p], z_recv.at[h, p])
            more = zr[h, p].astype(F32)
            total = more if i == 1 else total + more
        r_out[2, :, h * KH:(h + 1) * KH] = total
        r_out[3, :, h * KH:(h + 1) * KH] = zc[h, place]

    def right_products(h):
        for b in range(4):
            full = jnp.dot(vv[:, b * TILE:(b + 1) * TILE], om[b // 2, h, (b % 2) * TILE:(b % 2 + 1) * TILE, :],
                           preferred_element_type=F32)
            for a in range(2):
                piece = full[a * RMAX:(a + 1) * RMAX]
                cr[a, b * RMAX:(b + 1) * RMAX, :] = jnp.where(level < limit(a, b), piece, 0.0).astype(BF16)
        for a in range(2):
            yp[h, 4 * a:4 * a + 4] += jnp.dot(uu[a * TILE:(a + 1) * TILE, :], cr[a],
                                              preferred_element_type=F32).reshape(4, 2, 64, KH)
            b, off = ((3, 0), (0, 2))[a]

            @pl.when(corners[a, b])
            def _(a=a, b=b, off=off):
                add_right(h, a, b, tile(a, off))
            y16[h, 4 * a:4 * a + 4] = yp[h, 4 * a:4 * a + 4].astype(BF16)

    def send_right(h):
        for part in (1 - zh, zh):
            for i in range(1, 8):
                p = (y + i) % 8
                start(None, remote(y16.at[h, p, part], yr.at[h, y, part], y_send.at[h, part, i],
                                   y_recv.at[h, part, y], device(x, zl, k, p, zh)))

    def sum_right(h, part):
        total = yp[h, y, part]
        for i in range(1, 8):
            p = (y + i) % 8
            arrived(yr.at[h, p, part], y_recv.at[h, part, p])
            total += yr[h, p, part].astype(F32)
        return total

    def pass_right(h):
        yacc[h] = sum_right(h, 1 - zh)
        start(None, remote(yacc.at[h], yh.at[h], h_send.at[h], h_recv.at[h], device(x, zl, k, y, 1 - zh)))

    def end_right(h):
        total = sum_right(h, zh)
        arrived(yh.at[h], h_recv.at[h])
        r_out[0, :, h * KH:(h + 1) * KH] = total
        r_out[1, :, h * KH:(h + 1) * KH] = yh[h]

    scatter_omega(0)
    scatter_omega(1)
    relay_psi(0)
    relay_psi(1)
    send_psi(0,False)
    spread_omega(0,True)
    spread_omega(1,True)
    share_root()
    send_psi(0,True)
    pass_psi(0,False)
    spread_omega(0,False)
    send_psi(1,False)
    pass_psi(0,True)
    spread_omega(1,False)
    send_psi(1,True)
    pass_psi(1,False)
    pass_psi(1,True)
    for c in loads:
        c.wait()
    diagonal_products()
    share_omega(0)
    omega_arrived(0)
    right_products(0)
    send_right(0)
    psi_arrived(0)
    left_products(0)
    share_omega(1)
    send_left(0)
    omega_arrived(1)
    right_products(1)
    send_right(1)
    psi_arrived(1)
    left_products(1)
    rest = pending[:]
    send_left(1)
    late = pending[len(rest):]
    pending[:] = rest
    flush()
    pending[:] = late
    pass_right(0)
    pass_right(1)
    last = pending[-2:]
    del pending[-2:]
    sum_left(0)
    flush()
    pending[:] = last
    sum_left(1)
    end_right(0)
    end_right(1)

    flush()


def local(omega, psi, near_tiles, left_factors, right_factors, admissible, ranks):
    dma = pltpu.SemaphoreType.DMA
    anywhere = pl.BlockSpec(memory_space=pl.ANY)
    vmem = pl.BlockSpec(memory_space=pltpu.VMEM)
    out = jax.ShapeDtypeStruct((4, 64, K), F32)
    parts = pl.pallas_call(
        kernel,
        out_shape=out,
        in_specs=[anywhere] * 7,
        out_specs=vmem,
        scratch_shapes=[
            pltpu.VMEM((2, 2, 1024, KH), BF16),
            pltpu.VMEM((2, 1024, KH), BF16),
            pltpu.VMEM((2, 1024, KH), BF16),
            pltpu.VMEM((2, 256, KH), BF16),
            pltpu.VMEM((2, 2, 256, KH), BF16),
            pltpu.VMEM((1024, 3 * TILE), BF16),
            pltpu.VMEM((1024, 256), BF16),
            pltpu.VMEM((128, 2048), BF16),
            pltpu.VMEM((2, 256, KH), BF16),
            pltpu.VMEM((4, 128, KH), BF16),
            pltpu.VMEM((2, 8, 2, 64, KH), F32),
            pltpu.VMEM((2, 8, 2, 64, KH), BF16),
            pltpu.VMEM((2, 8, 2, 64, KH), BF16),
            pltpu.VMEM((2, 64, KH), F32),
            pltpu.VMEM((2, 64, KH), F32),
            pltpu.VMEM((2, 16, 2, 64, KH), F32),
            pltpu.VMEM((2, 16, 64, KH), F32),
            pltpu.VMEM((2, 16, 64, KH), BF16),
            pltpu.VMEM((2, 16, 64, KH), BF16),
            pltpu.SMEM((2, 4), jnp.int32),
            pltpu.SMEM((2, 4), jnp.int32),
            dma((11,)), dma((2,)), dma((2,)), dma((2, 2)), dma((2, 2)), dma((2, 9)), dma((2, 4)), dma((2, 9)), dma((2, 4)), dma((2, 4)), dma((2, 4)),
            dma((2, 2, 8)), dma((2, 2, 8)), dma((2,)), dma((2,)), dma((2, 4)), dma((2, 4)),
            dma((2, 16)), dma((2, 16)),
        ],
        compiler_params=pltpu.CompilerParams(collective_id=0, has_side_effects=True,
                                             vmem_limit_bytes=64 << 20),
        cost_estimate=pl.CostEstimate(flops=2 * 10 ** 9, bytes_accessed=6 << 20, transcendentals=0),
    )(omega, psi, near_tiles, left_factors, right_factors, admissible, ranks)
    return (parts[0] + parts[1], parts[2] + parts[3])


def solution(mesh):
    return jax.shard_map(
        local,
        mesh=mesh,
        in_specs=(
            P("row", None),
            P("col", None),
            P("row", None),
            P("row", "col"),
            P("row", "col"),
            P("row", "col"),
            P("row", "col"),
        ),
        out_specs=(P(("row", "col"), None), P(("col", "row"), None)),
        check_vma=False,
    )
```
